32 devices in a mesh: blk: 8 (over z, x), batch: 4 (over y, core).
Axes of the slice: x: 2, y: 2, z: 4, core: 2. Of those that a mesh axis runs over, the one named last changes fastest.
Arguments:
- byte_states: bfloat16 [8, 1024, 512], P('batch', 'blk'), may hold values from -6 to 6
- word_start: int32 [8, 1024], P('batch', 'blk'), may hold values from 0 to 1023, as said below
- bucket_of: int32 [2047], replicated, may hold values from 0 to 31, as said below
- conv_two: bfloat16 [2, 512], replicated, may hold values from -4 to 4
- conv_three: bfloat16 [3, 512], replicated, may hold values from -4 to 4
- conv_four: bfloat16 [4, 512], replicated, may hold values from -4 to 4
- w_join: bfloat16 [512, 512], replicated, may hold values from -0.25 to 0.25
- norm_attn: bfloat16 [512], replicated, may hold values from 0.25 to 1.75
- w_query: bfloat16 [512, 512], replicated, may hold values from -0.0625 to 0.0625
- w_key: bfloat16 [512, 512], replicated, may hold values from -0.25 to 0.25
- w_value: bfloat16 [512, 512], replicated, may hold values from -0.25 to 0.25
- w_out: bfloat16 [512, 512], replicated, may hold values from -1.5 to 1.5
- rel_bias: bfloat16 [32, 8], replicated, may hold values from -4 to 4
- norm_ffn: bfloat16 [512], replicated, may hold values from 0.25 to 1.75
- w_gate: bfloat16 [512, 2048], replicated, may hold values from -0.25 to 0.25
- w_up: bfloat16 [512, 2048], replicated, may hold values from -0.25 to 0.25
- w_down: bfloat16 [2048, 512], replicated, may hold values from -0.125 to 0.125
- grad_output: bfloat16 [8, 1024, 512], P('batch', 'blk'), may hold values from -6 to 6
Outputs:
- output: bfloat16 [8, 1024, 512], P('batch', 'blk')
- grad_states: float32 [8, 1024, 512], P('batch', 'blk')
- grad_conv_two: float32 [2, 512], replicated
- grad_conv_three: float32 [3, 512], replicated
- grad_conv_four: float32 [4, 512], replicated
- grad_w_join: float32 [512, 512], replicated
- grad_norm_attn: float32 [512], replicated
- grad_w_query: float32 [512, 512], replicated
- grad_w_key: float32 [512, 512], replicated
- grad_w_value: float32 [512, 512], replicated
- grad_w_out: float32 [512, 512], replicated
- grad_rel_bias: float32 [32, 8], replicated
- grad_norm_ffn: float32 [512], replicated
- grad_w_gate: float32 [512, 2048], replicated
- grad_w_up: float32 [512, 2048], replicated
- grad_w_down: float32 [2048, 512], replicated
The draws below stay inside these ranges and needn't reach their ends.
Inputs may be any that keep to these rules, and one draw needn't show every extreme that they name: word_start[b, t] is at most t, equals t or word_start[b, t - 1], and is 0 at t = 0; a word never begins at a byte t > 0 with t % 128 == 0; the last byte of every sequence is a word of its own. bucket_of[r + 1023] is the bucket of a key r places after its query: buckets 0 to 15 for r <= 0, the others for r > 0; on each side the bucket never falls as |r| grows, and each |r| below 8 has a bucket of its own.
All inputs are finite; a program needn't handle non-finite values.
Results may differ from the reference program's by a relative error of at most 0.018.
Values may be sent and summed in bfloat16 or wider, within the bound.
No kernel may reach another device: no remote copies, remote signals or barrier semaphores. Data moves between devices by JAX's collectives and lax.ppermute only.
A program may use at most 128 MiB of HBM per device.

```python
import math
import jax
import jax.numpy as jnp
from jax import lax

D = 512
HEADS = 8
HEAD_DIM = 64
FF = 2048
BUCKETS = 32
BYTES_DEV = 128
LENGTH = 1024
BATCH = 8


def draw_word_start(key, part):
    key = jax.random.fold_in(key, 11)
    word_flags = jax.random.randint(key, (BATCH, LENGTH), 0, 5) == 0
    positions = jnp.arange(LENGTH, dtype=jnp.int32)
    word_flags = word_flags & (positions[None, :] % BYTES_DEV != 0)
    word_flags = word_flags | (positions[None, :] == 0) | (positions[None, :] == LENGTH - 1)
    starts = jnp.where(word_flags, positions[None, :], 0).astype(jnp.int32)
    return lax.cummax(starts, axis=1).astype(jnp.int32)


def side_breaks(side_key):
    quarter = BUCKETS // 4
    far_picks = jax.random.permutation(side_key, LENGTH - quarter)[:quarter].astype(jnp.int32) + quarter
    return jnp.concatenate([jnp.arange(1, quarter, dtype=jnp.int32), jnp.sort(far_picks).astype(jnp.int32)])


def draw_bucket_of(key, part):
    key = jax.random.fold_in(key, 23)
    near_key, far_key = jax.random.split(key)
    relative = jnp.arange(2 * LENGTH - 1, dtype=jnp.int32) - (LENGTH - 1)
    distance = jnp.abs(relative)
    below_count = jnp.sum((distance[:, None] >= side_breaks(near_key)[None, :]).astype(jnp.int32), axis=1).astype(jnp.int32)
    above_count = jnp.sum((distance[:, None] >= side_breaks(far_key)[None, :]).astype(jnp.int32), axis=1).astype(jnp.int32)
    return jnp.where(relative > 0, BUCKETS // 2 + above_count, below_count).astype(jnp.int32)


def shard_levels(stream_key, extent, cuts, least, high):
    def one(dim, blocks):
        heights = jax.random.uniform(jax.random.fold_in(jax.random.fold_in(stream_key, 6), dim), (blocks,), jnp.float32, least / len(cuts), high / len(cuts))
        return jnp.repeat(jnp.exp(heights), extent[dim] // blocks).reshape((-1,) + (1,) * (len(extent) - dim - 1))

    factor_of = one(*cuts[0])
    for cut in cuts[1:]:
        factor_of = factor_of * one(*cut)
    return factor_of


def normal_values(own_key, extent, spread, most, shards=(), held_as=jnp.bfloat16):
    level = shard_levels(own_key, extent, shards, -0.22, 0.18) if shards else 1.0
    array = jax.random.normal(own_key, extent, jnp.float32) * spread * level
    return jnp.minimum(jnp.maximum(array, -most), most).astype(held_as)


def setup_inputs(seed: int = 0) -> dict:
    streams_of = jax.random.split(jax.random.key(seed), 19)
    return {
        "byte_states": normal_values(streams_of[0], (BATCH, LENGTH, D), 1.0, 6.0, ((0, 4), (1, 8))),
        "word_start": draw_word_start(jax.random.fold_in(streams_of[18], 71), 0),
        "bucket_of": draw_bucket_of(jax.random.fold_in(streams_of[18], 71), 0),
        "conv_two": normal_values(streams_of[3], (2, D), 0.3, 4.0),
        "conv_three": normal_values(streams_of[4], (3, D), 0.3, 4.0),
        "conv_four": normal_values(streams_of[5], (4, D), 0.3, 4.0),
        "w_join": normal_values(streams_of[6], (D, D), D ** -0.5, 0.25),
        "norm_attn": jnp.clip(1.0 + 0.15 * jax.random.normal(streams_of[7], (D,), jnp.float32), 0.25, 1.75).astype(jnp.bfloat16),
        "w_query": normal_values(streams_of[8], (D, D), (16 * D) ** -0.5, 0.0625),
        "w_key": normal_values(streams_of[9], (D, D), D ** -0.5, 0.25),
        "w_value": normal_values(streams_of[10], (D, D), D ** -0.5, 0.25),
        "w_out": normal_values(streams_of[11], (D, D), (D // 32) ** -0.5, 1.5),
        "rel_bias": normal_values(streams_of[12], (BUCKETS, HEADS), 1.0, 4.0),
        "norm_ffn": jnp.clip(1.0 + 0.15 * jax.random.normal(streams_of[13], (D,), jnp.float32), 0.25, 1.75).astype(jnp.bfloat16),
        "w_gate": normal_values(streams_of[14], (D, FF), D ** -0.5, 0.25),
        "w_up": normal_values(streams_of[15], (D, FF), D ** -0.5, 0.25),
        "w_down": normal_values(streams_of[16], (FF, D), FF ** -0.5, 0.125),
        "grad_output": normal_values(streams_of[17], (BATCH, LENGTH, D), 1.0, 6.0, ((0, 4), (1, 8))),
    }


@jax.custom_vjp
def low(v):
    return lax.optimization_barrier(v.astype(jnp.bfloat16)).astype(jnp.float32)

@jax.custom_vjp
def low_back(v):
    return v

def low_keep(v):
    return (low(v), None)

def low_pass(kept, grad):
    return (grad,)

def back_keep(v):
    return (v, None)

def back_low(kept, grad):
    return (low(grad),)
low.defvjp(low_keep, low_pass)
low_back.defvjp(back_keep, back_low)
norm_eps = 1e-06

def matmul(left_side, right_side):
    return jnp.matmul(left_side, right_side, precision=lax.Precision.HIGHEST)

def rms_scale(values, gain_vec):
    return values * lax.rsqrt(lax.optimization_barrier(jnp.mean(values * values, axis=-1, keepdims=True)) + norm_eps) * gain_vec

def gelu_tanh(values):
    return jax.nn.gelu(values, approximate=True)

def reference(byte_states, word_start, bucket_of, conv_two, conv_three, conv_four, w_join, norm_attn, w_query, w_key, w_value, w_out, rel_bias, norm_ffn, w_gate, w_up, w_down, grad_output):
    positions = jnp.arange(LENGTH, dtype=jnp.int32)
    block_rows = math.gcd(LENGTH, 512)
    per_sequence = LENGTH // block_rows
    block_count = BATCH * per_sequence

    def forward(params, states):
        c_two, c_three, c_four, join_proj, gain_attn, proj_q, proj_k, proj_v, proj_o, bias_table, gain_ffn, proj_g, proj_u, proj_d = params
        tap_list = [c_two[0] + c_three[0] + c_four[0], c_two[1] + c_three[1] + c_four[1], c_three[2] + c_four[2], c_four[3]]
        ngram_sum = jnp.zeros_like(states)
        for offset in range(4):
            moved_rows = jnp.pad(states, ((0, 0), (offset, 0), (0, 0)))[:, :LENGTH, :]
            keep_mask = (positions[None, :] - offset >= word_start).astype(jnp.float32)
            ngram_sum = ngram_sum + tap_list[offset] * keep_mask[:, :, None] * moved_rows
        joined_states = states + low_back(matmul(low(ngram_sum), join_proj))
        normed = low(rms_scale(joined_states, gain_attn))
        query_all = low(low_back(matmul(normed, proj_q))).reshape(BATCH, LENGTH, HEADS, HEAD_DIM)
        key_all = low(low_back(matmul(normed, proj_k))).reshape(BATCH, LENGTH, HEADS, HEAD_DIM)
        value_all = low(low_back(matmul(normed, proj_v))).reshape(BATCH, LENGTH, HEADS, HEAD_DIM)

        def attend(block_id):
            zero_index = jnp.zeros((), jnp.int32)
            seq_index = (block_id // per_sequence).astype(jnp.int32)
            row_start = (block_id % per_sequence * block_rows).astype(jnp.int32)
            query_rows = lax.dynamic_slice(query_all, (seq_index, row_start, zero_index, zero_index), (1, block_rows, HEADS, HEAD_DIM))[0]
            key_rows = lax.dynamic_index_in_dim(key_all, seq_index, 0, keepdims=False)
            value_rows = lax.dynamic_index_in_dim(value_all, seq_index, 0, keepdims=False)
            query_pos = row_start + jnp.arange(block_rows, dtype=jnp.int32)
            buckets = bucket_of[positions[None, :] - query_pos[:, None] + LENGTH - 1]
            pair_bias = jnp.transpose(bias_table[buckets], (2, 0, 1))
            scores = jnp.einsum('qhd,khd->hqk', query_rows, key_rows, precision=lax.Precision.HIGHEST)
            scores = low_back(scores + pair_bias)
            weight = jnp.exp(scores)
            weight_sum = lax.optimization_barrier(jnp.sum(weight, axis=-1))
            mixed_sum = low_back(jnp.einsum('hqk,khd->qhd', low(weight), value_rows, precision=lax.Precision.HIGHEST))
            return mixed_sum / jnp.transpose(weight_sum)[:, :, None]
        attended = lax.map(jax.checkpoint(attend), jnp.arange(block_count, dtype=jnp.int32))
        attended = attended.reshape(BATCH, LENGTH, HEADS * HEAD_DIM)
        mid_states = joined_states + low_back(matmul(low(attended), proj_o))
        normed_ffn = low(rms_scale(mid_states, gain_ffn))
        gate_proj = low_back(matmul(normed_ffn, proj_g))
        up_proj = low_back(matmul(normed_ffn, proj_u))
        hidden = low(gelu_tanh(gate_proj) * up_proj)
        return mid_states + matmul(hidden, proj_d)
    params = tuple((weight_arg.astype(jnp.float32) for weight_arg in (conv_two, conv_three, conv_four, w_join, norm_attn, w_query, w_key, w_value, w_out, rel_bias, norm_ffn, w_gate, w_up, w_down)))
    output, pullback = jax.vjp(forward, params, byte_states.astype(jnp.float32))
    param_grads, grad_states = pullback(grad_output.astype(jnp.float32))
    return (output.astype(jnp.bfloat16), grad_states, param_grads[0], param_grads[1], param_grads[2], param_grads[3], param_grads[4], param_grads[5], param_grads[6], param_grads[7], param_grads[8], param_grads[9], param_grads[10], param_grads[11], param_grads[12], param_grads[13])
```

```python
from functools import partial

import jax
import jax.numpy as jnp
from jax import lax
from jax.experimental import pallas as pl
from jax.experimental.pallas import tpu as pltpu
from jax.sharding import PartitionSpec as P

norm_eps = 1e-06
LANES = 128
EDGE = 3
CHUNKS = 4
KEY_BLOCKS = 4
VMEM_LIMIT = 65400 * 1024
GELU_SCALE = 0.7978845608028654
GELU_CUBE = 0.044715


def lasting(micros):
    return pl.CostEstimate(flops=0, transcendentals=0, bytes_accessed=int(micros * 3.5e6))


IN_HBM = pl.BlockSpec(memory_space=pltpu.HBM)


def shifted(block, axis, distance):
    devices = range(lax.axis_size(axis))
    route = [(i - distance, i) for i in devices if i - distance in devices]
    return lax.ppermute(block, axis, route)


def project(left_side, right_side):
    return jnp.dot(left_side, right_side, preferred_element_type=jnp.float32)


def project_back(left_side, right_side):
    return lax.dot_general(
        left_side, right_side, (((1,), (1,)), ((), ())), preferred_element_type=jnp.float32
    )


def over_rows(left_side, right_side):
    return lax.dot_general(
        left_side, right_side, (((0,), (0,)), ((), ())), preferred_element_type=jnp.float32
    )


def turned(low_block):
    return jnp.transpose(low_block.astype(jnp.float32)).astype(jnp.bfloat16)


def inverse_rms(values):
    return lax.rsqrt(jnp.mean(values * values, axis=-1, keepdims=True) + norm_eps)


def rms_back(values, gain, grad):
    scale = inverse_rms(values)
    scaled = values * scale
    gained = gain * grad
    lean = jnp.mean(scaled * gained, axis=-1, keepdims=True)
    return scale * (gained - scaled * lean), jnp.sum(grad * scaled, axis=0, keepdims=True)


def tap_rows(two_ref, three_ref, four_ref):
    two, three, four = (r[...].astype(jnp.float32) for r in (two_ref, three_ref, four_ref))
    return [
        two[0:1] + three[0:1] + four[0:1],
        two[1:2] + three[1:2] + four[1:2],
        three[2:3] + four[2:3],
        four[3:4],
    ]


def keep_columns(start_ref, sequence, first, rows, width):
    starts = jnp.transpose(
        jnp.broadcast_to(start_ref[sequence : sequence + 1, :].astype(jnp.float32), (rows, rows))
    )
    spots = (lax.broadcasted_iota(jnp.int32, (rows, rows), 0) + first).astype(jnp.float32)
    lead = spots - starts
    return [
        jnp.concatenate([(lead >= float(j)).astype(jnp.float32)] * (width // rows), axis=1)
        for j in range(4)
    ]


def front_kernel(*refs, sequences, rows, heads, dim, count):
    width = heads * dim
    given, made, held = refs[:count], refs[count : count + 4], refs[count + 4 : 2 * count + 4]
    joined_ref, normed_ref, ngram_ref, sent_ref, ext_ref, sems = refs[2 * count + 4 :]
    waiting = copies_between(given, held, sems)
    (states_ref, rim_ref, start_ref, two_ref, three_ref, four_ref, wjoin_ref, gain_ref, wq_ref, wk_ref,
     wv_ref) = held
    for copy in waiting[:6]:
        copy.wait()
    taps = tap_rows(two_ref, three_ref, four_ref)
    for s in range(sequences):
        span = slice(s * rows, (s + 1) * rows)
        states = states_ref[s].astype(jnp.float32)
        ext_ref[8 - EDGE : 8, :] = rim_ref[s].astype(jnp.float32)
        ext_ref[8 : 8 + rows, :] = states
        keeps = keep_columns(start_ref, s, lax.axis_index("blk") * rows, rows, width)
        ngram = taps[0] * keeps[0] * states
        for j in range(1, 4):
            ngram = ngram + taps[j] * keeps[j] * ext_ref[8 - j : 8 - j + rows, :]
        low = ngram.astype(jnp.bfloat16)
        ngram_ref[span, :] = low
        if s == 0:
            waiting[6].wait()
        joined_ref[span, :] = states + project(low, wjoin_ref[...])
    done = copies_between((joined_ref, ngram_ref), (made[0], made[2]), sems, count)
    waiting[7].wait()
    joined = joined_ref[...]
    gain = gain_ref[...].astype(jnp.float32).reshape(1, -1)
    normed = (joined * inverse_rms(joined) * gain).astype(jnp.bfloat16)
    normed_ref[...] = normed
    done += copies_between((normed_ref,), (made[1],), sems, count + 2)
    for part, w_ref in enumerate((wq_ref, wk_ref, wv_ref)):
        waiting[8 + part].wait()
        flipped = jnp.transpose(project(normed, w_ref[...])).astype(jnp.bfloat16)
        features = pl.ds(part * dim, dim)
        for h in range(heads):
            for s in range(sequences):
                unit = h * sequences + s
                per_block = sent_ref.shape[1]
                sent_ref[unit // per_block, unit % per_block, part * dim : (part + 1) * dim, :] = flipped[
                    h * dim : (h + 1) * dim, s * rows : (s + 1) * rows
                ]
        done += copies_between(
            (sent_ref.at[:, :, features, :],), (made[3].at[:, :, features, :],), sems, count + 3 + part
        )
    for copy in done:
        copy.wait()


def whole(shape):
    return pl.BlockSpec(shape, lambda *_: (0,) * len(shape))


def front(states, rim, starts, two, three, four, w_join, gain, w_query, w_key, w_value, heads, blocks):
    sequences, rows, width = states.shape
    dim = width // heads
    flat = sequences * rows
    operands = (states, rim, starts, two, three, four, w_join, gain, w_query, w_key, w_value)
    outs = [
        jax.ShapeDtypeStruct((flat, width), jnp.float32),
        jax.ShapeDtypeStruct((flat, width), jnp.bfloat16),
        jax.ShapeDtypeStruct((flat, width), jnp.bfloat16),
        jax.ShapeDtypeStruct((blocks, heads * sequences // blocks, 3 * dim, rows), jnp.bfloat16),
    ]
    count = len(operands)
    return pl.pallas_call(
        partial(front_kernel, sequences=sequences, rows=rows, heads=heads, dim=dim, count=count),
        in_specs=[IN_HBM] * count,
        out_specs=[IN_HBM] * len(outs),
        out_shape=outs,
        scratch_shapes=held_here(operands) + held_here(outs) + [
            pltpu.VMEM((8 + rows, width), jnp.float32), pltpu.SemaphoreType.DMA((count + 6,)),
        ],
        compiler_params=pltpu.CompilerParams(vmem_limit_bytes=VMEM_LIMIT),
        cost_estimate=lasting(3.8),
        name="front",
    )(*operands)


def joined_blocks(ref, unit, first, count, low, high):
    return jnp.concatenate(
        [ref[first + i, unit, low:high, :] for i in range(count)], axis=1
    )


def unit_head(held, sequences):
    return (lax.axis_index("blk") * held + pl.program_id(0)) // sequences


def attend_kernel(
    qkv_ref, bucket_ref, table_ref, weight_ref, low_ref, att_ref, total_ref, toep_ref, key_ref,
    *, blocks, rows, dim, tile, held, sequences,
):
    length = blocks * rows
    step = pl.program_id(1)
    per_tile = tile // rows

    @pl.when(step == 0)
    def _():
        buckets = table_ref.shape[1]
        hot = lax.broadcasted_iota(jnp.int32, (buckets, 2 * length), 0) == bucket_ref[...]
        own = lax.broadcasted_iota(jnp.int32, table_ref.shape, 0) == unit_head(held, sequences)
        row = jnp.sum(jnp.where(own, table_ref[...].astype(jnp.float32), 0.0), axis=0, keepdims=True)
        square = (buckets, buckets)
        same = lax.broadcasted_iota(jnp.int32, square, 0) == lax.broadcasted_iota(jnp.int32, square, 1)
        column = jnp.sum(jnp.where(same, row, 0.0), axis=1, keepdims=True)
        line = jnp.sum(jnp.where(hot, column, 0.0), axis=0, keepdims=True)
        spread_line = jnp.broadcast_to(line, (rows, 2 * length))
        toep_ref[...] = pltpu.roll(spread_line, 0, 1, stride=1, stride_axis=0)
        for j in range(blocks):
            key_ref[rows * j : rows * (j + 1), :] = turned(qkv_ref[j, 0, dim : 2 * dim, :])

    query_t = joined_blocks(qkv_ref, 0, step * per_tile, per_tile, 0, dim)
    total = jnp.zeros((1, tile), jnp.float32)
    mix = jnp.zeros((dim, tile), jnp.float32)
    group = min(KEY_BLOCKS, blocks)
    for j in range(0, blocks, group):
        value_t = joined_blocks(qkv_ref, 0, j, group, 2 * dim, 3 * dim)
        bias = jnp.concatenate(
            [
                toep_ref[:, pl.ds(pl.multiple_of(length - rows + step * tile - rows * i, LANES), tile)]
                for i in range(j, j + group)
            ],
            axis=0,
        )
        span = slice(rows * j, rows * (j + group))
        weight = jnp.exp(project(key_ref[span, :], query_t) + bias)
        total = total + jnp.sum(weight, axis=0, keepdims=True)
        weight_low = weight.astype(jnp.bfloat16)
        weight_ref[0, span, :] = weight_low
        mix = mix + project(value_t, weight_low)
    att = mix / total
    att_ref[0] = att
    total_ref[0] = total
    att_low = att.astype(jnp.bfloat16)
    for i in range(per_tile):
        low_ref[i, 0] = att_low[:, i * rows : (i + 1) * rows]


def attend_back_kernel(
    qkv_ref, weight_ref, att_ref, total_ref, grad_ref, bucket_ref, out_ref, table_ref,
    diag_ref, gkey_ref, gvalue_ref, value_ref, *, blocks, rows, dim, tile, held, sequences,
):
    length = blocks * rows
    step = pl.program_id(1)
    per_tile = tile // rows

    @pl.when(step + pl.program_id(0) == 0)
    def _():
        table_ref[...] = jnp.zeros_like(table_ref)

    @pl.when(step == 0)
    def _():
        diag_ref[...] = jnp.zeros_like(diag_ref)
        gkey_ref[...] = jnp.zeros_like(gkey_ref)
        gvalue_ref[...] = jnp.zeros_like(gvalue_ref)
        for j in range(blocks):
            value_ref[rows * j : rows * (j + 1), :] = turned(qkv_ref[j, 0, 2 * dim : 3 * dim, :])

    query_t = joined_blocks(qkv_ref, 0, step * per_tile, per_tile, 0, dim)
    query = jnp.transpose(query_t.astype(jnp.float32)).astype(jnp.bfloat16)
    grad_att = joined_blocks(grad_ref, 0, 0, per_tile, 0, dim).astype(jnp.float32)
    inverse = 1.0 / total_ref[0]
    shift = jnp.sum(grad_att * att_ref[0], axis=0, keepdims=True) * inverse
    scaled = grad_att * inverse
    mix_t = scaled.astype(jnp.bfloat16)
    mix = jnp.transpose(scaled).astype(jnp.bfloat16)
    gquery = jnp.zeros((dim, tile), jnp.float32)
    group = min(KEY_BLOCKS, blocks)
    for j in range(0, blocks, group):
        span = slice(rows * j, rows * (j + group))
        key_t = joined_blocks(qkv_ref, 0, j, group, dim, 2 * dim)
        weight_low = weight_ref[0, span, :]
        grad_weight = project(value_ref[span, :], mix_t)
        grad_score = weight_low.astype(jnp.float32) * (grad_weight - shift)
        score_low = grad_score.astype(jnp.bfloat16)
        for i in range(group):
            start = pl.multiple_of(length - rows + step * tile - rows * (j + i), LANES)
            diag_ref[:, pl.ds(start, tile)] += grad_score[rows * i : rows * (i + 1)]
        gquery = gquery + project(key_t, score_low)
        gkey_ref[span, :] += project(score_low, query)
        gvalue_ref[span, :] += project(weight_low, mix)
    gquery_low = gquery.astype(jnp.bfloat16)
    for i in range(per_tile):
        out_ref[step * per_tile + i, 0, 0:dim, :] = gquery_low[:, i * rows : (i + 1) * rows]

    @pl.when(step == pl.num_programs(1) - 1)
    def _():
        for j in range(blocks):
            span = slice(rows * j, rows * (j + 1))
            out_ref[j, 0, dim : 2 * dim, :] = jnp.transpose(gkey_ref[span, :]).astype(jnp.bfloat16)
            out_ref[j, 0, 2 * dim : 3 * dim, :] = jnp.transpose(gvalue_ref[span, :]).astype(
                jnp.bfloat16
            )
        width = 2 * length
        part = diag_ref[...]
        half = rows // 2
        while half >= 8:
            part = part[:half] + pltpu.roll(part[half:], width - half, 1)
            half //= 2
        line = part[0:1]
        for r in range(1, 8):
            line = line + pltpu.roll(part[r : r + 1], width - r, 1)
        buckets = table_ref.shape[0]
        hot = lax.broadcasted_iota(jnp.int32, (buckets, width), 0) == bucket_ref[...]
        sums = jnp.sum(jnp.where(hot, line, 0.0), axis=1, keepdims=True)
        own = lax.broadcasted_iota(jnp.int32, table_ref.shape, 1) == unit_head(held, sequences)
        table_ref[...] += jnp.where(own, sums, 0.0)


def attend(qkv, bucket_line, table, blocks, rows, dim, tile, sequences):
    units = qkv.shape[1]
    length = blocks * rows
    per_tile = tile // rows
    return pl.pallas_call(
        partial(
            attend_kernel, blocks=blocks, rows=rows, dim=dim, tile=tile, held=units, sequences=sequences
        ),
        grid=(units, length // tile),
        in_specs=[
            pl.BlockSpec((blocks, 1, 3 * dim, rows), lambda u, i: (0, u, 0, 0)),
            pl.BlockSpec((1, 2 * length), lambda u, i: (0, 0)),
            whole(table.shape),
        ],
        out_specs=[
            pl.BlockSpec((1, length, tile), lambda u, i: (u, 0, i)),
            pl.BlockSpec((per_tile, 1, dim, rows), lambda u, i: (i, u, 0, 0)),
            pl.BlockSpec((1, dim, tile), lambda u, i: (u, 0, i)),
            pl.BlockSpec((1, 1, tile), lambda u, i: (u, 0, i)),
        ],
        out_shape=[
            jax.ShapeDtypeStruct((units, length, length), jnp.bfloat16),
            jax.ShapeDtypeStruct((blocks, units, dim, rows), jnp.bfloat16),
            jax.ShapeDtypeStruct((units, dim, length), jnp.float32),
            jax.ShapeDtypeStruct((units, 1, length), jnp.float32),
        ],
        scratch_shapes=[
            pltpu.VMEM((rows, 2 * length), jnp.float32), pltpu.VMEM((length, dim), jnp.bfloat16),
        ],
        compiler_params=pltpu.CompilerParams(vmem_limit_bytes=VMEM_LIMIT),
        cost_estimate=lasting(7),
        name="attend",
    )(qkv, bucket_line, table)


def attend_back(
    qkv, weight, att, total, grad_att, bucket_line, buckets, blocks, rows, dim, tile, sequences
):
    units = qkv.shape[1]
    length = blocks * rows
    per_tile = tile // rows
    return pl.pallas_call(
        partial(
            attend_back_kernel, blocks=blocks, rows=rows, dim=dim, tile=tile, held=units,
            sequences=sequences,
        ),
        grid=(units, length // tile),
        in_specs=[
            pl.BlockSpec((blocks, 1, 3 * dim, rows), lambda u, i: (0, u, 0, 0)),
            pl.BlockSpec((1, length, tile), lambda u, i: (u, 0, i)),
            pl.BlockSpec((1, dim, tile), lambda u, i: (u, 0, i)),
            pl.BlockSpec((1, 1, tile), lambda u, i: (u, 0, i)),
            pl.BlockSpec((per_tile, 1, dim, rows), lambda u, i: (i, u, 0, 0)),
            pl.BlockSpec((1, 2 * length), lambda u, i: (0, 0)),
        ],
        out_specs=[
            pl.BlockSpec((blocks, 1, 3 * dim, rows), lambda u, i: (0, u, 0, 0)),
            whole((buckets, LANES)),
        ],
        out_shape=[
            jax.ShapeDtypeStruct((blocks, units, 3 * dim, rows), jnp.bfloat16),
            jax.ShapeDtypeStruct((buckets, LANES), jnp.float32),
        ],
        scratch_shapes=[
            pltpu.VMEM((rows, 2 * length), jnp.float32),
            pltpu.VMEM((length, dim), jnp.float32),
            pltpu.VMEM((length, dim), jnp.float32),
            pltpu.VMEM((length, dim), jnp.bfloat16),
        ],
        compiler_params=pltpu.CompilerParams(vmem_limit_bytes=VMEM_LIMIT),
        cost_estimate=lasting(12),
        name="attend_back",
    )(qkv, weight, att, total, grad_att, bucket_line)


def unit_columns(parts_ref, sequences, heads, low, high):
    held = parts_ref.shape[1]

    def part(unit):
        return parts_ref[unit // held, unit % held, low:high, :]

    return jnp.concatenate(
        [
            jnp.concatenate([part(h * sequences + s) for h in range(heads)], axis=0)
            for s in range(sequences)
        ],
        axis=1,
    )


def middle_kernel(*refs, sequences, rows, heads, dim, count, chunks):
    given, made, held = refs[:count], refs[count : count + 7], refs[count + 7 : 2 * count + 7]
    out_ref, normed_ref, keep_ref, send_ref, gmid_ref, gsent_ref, ggain_ref = refs[2 * count + 7 : 2 * count + 14]
    total_ref, gnormed_ref, sems = refs[2 * count + 14 :]
    parts_ref, joined_ref, wout_ref, gain_ref, grad_ref, wgate_ref, wup_ref, wdown_ref = held
    half = chunks // 2
    piece = wgate_ref.shape[1] // chunks
    first = lax.axis_index("batch") % 2 * half
    spans = [pl.ds(pl.multiple_of((first + i) % chunks * piece, piece), piece) for i in range(chunks)]
    waiting = copies_between(given[:5], held[:5], sems)
    for i, span in enumerate(spans):
        pairs = [(given[5].at[:, span], wgate_ref.at[:, span]), (given[6].at[:, span], wup_ref.at[:, span]),
                 (given[7].at[span, :], wdown_ref.at[span, :])]
        waiting += copies_between([a for a, _ in pairs], [b for _, b in pairs], sems, 5 + 3 * i)
    used = 5 + 3 * chunks
    done = []

    def give(targets, sources):
        done.extend(copies_between(sources, targets, sems, used + len(done)))

    for copy in waiting[:5]:
        copy.wait()
    gain = gain_ref[...].astype(jnp.float32).reshape(1, -1)
    grad = grad_ref[...]
    att = turned(unit_columns(parts_ref, sequences, heads, 0, dim))
    mid = joined_ref[...] + project(att, wout_ref[...])
    joined_ref[...] = mid
    normed = (mid * inverse_rms(mid) * gain).astype(jnp.bfloat16)
    normed_ref[...] = normed
    give((made[1],), (normed_ref,))
    total_ref[...] = mid
    gnormed_ref[...] = jnp.zeros_like(gnormed_ref)
    for i, span in enumerate(spans):
        for copy in waiting[5 + 3 * i : 8 + 3 * i]:
            copy.wait()
        wgate, wup, wdown = wgate_ref[:, span], wup_ref[:, span], wdown_ref[span, :]
        gate = project(normed, wgate)
        up = project(normed, wup)
        square = gate * gate
        bend = jnp.tanh(GELU_SCALE * gate * (1.0 + GELU_CUBE * square))
        half_up = 0.5 + 0.5 * bend
        gelu = gate * half_up
        slope = half_up + 0.5 * gate * (1.0 - bend * bend) * (
            GELU_SCALE + (3.0 * GELU_SCALE * GELU_CUBE) * square
        )
        hidden = (gelu * up).astype(jnp.bfloat16)
        total_ref[...] += project(hidden, wdown)
        ghidden = project_back(grad, wdown)
        ggate = (ghidden * up * slope).astype(jnp.bfloat16)
        gup = (ghidden * gelu).astype(jnp.bfloat16)
        ref, target = (keep_ref, made[2]) if i < half else (send_ref, made[3])
        for part, block in enumerate((ggate, gup, hidden)):
            ref[i % half, part] = block
        give((target.at[i % half],), (ref.at[i % half],))
        gnormed_ref[...] += project_back(ggate, wgate) + project_back(gup, wup)
    out_ref[...] = total_ref[...].astype(jnp.bfloat16)
    give((made[0],), (out_ref,))
    back, ggain = rms_back(joined_ref[...], gain, gnormed_ref[...])
    gmid = grad.astype(jnp.float32) + back
    gmid_ref[...] = gmid
    ggain_ref[...] = ggain
    give((made[4], made[6]), (gmid_ref, ggain_ref))
    gatt = project_back(wout_ref[...], gmid.astype(jnp.bfloat16)).astype(jnp.bfloat16)
    for h in range(heads):
        for s in range(sequences):
            unit = h * sequences + s
            per_block = gsent_ref.shape[1]
            gsent_ref[unit // per_block, unit % per_block] = gatt[
                h * dim : (h + 1) * dim, s * rows : (s + 1) * rows
            ]
    give((made[5],), (gsent_ref,))
    for copy in done:
        copy.wait()


def middle(parts, joined, w_out, gain, w_gate, w_up, w_down, grad, sequences, heads, chunks):
    dim, rows = parts.shape[2:]
    flat, width = joined.shape
    piece = w_gate.shape[1] // chunks
    acts = (chunks // 2, 3, flat, piece)
    operands = (parts, joined, w_out, gain, grad, w_gate, w_up, w_down)
    outs = [
        jax.ShapeDtypeStruct((flat, width), jnp.bfloat16),
        jax.ShapeDtypeStruct((flat, width), jnp.bfloat16),
        jax.ShapeDtypeStruct(acts, jnp.bfloat16),
        jax.ShapeDtypeStruct(acts, jnp.bfloat16),
        jax.ShapeDtypeStruct((flat, width), jnp.float32),
        jax.ShapeDtypeStruct(parts.shape, jnp.bfloat16),
        jax.ShapeDtypeStruct((1, width), jnp.float32),
    ]
    count = len(operands)
    return pl.pallas_call(
        partial(
            middle_kernel, sequences=sequences, rows=rows, heads=heads, dim=dim, count=count, chunks=chunks
        ),
        in_specs=[IN_HBM] * count,
        out_specs=[IN_HBM] * len(outs),
        out_shape=outs,
        scratch_shapes=held_here(operands) + held_here(outs) + [
            pltpu.VMEM((flat, width), jnp.float32), pltpu.VMEM((flat, width), jnp.float32),
            pltpu.SemaphoreType.DMA((5 + 3 * chunks + 6 + chunks,)),
        ],
        compiler_params=pltpu.CompilerParams(vmem_limit_bytes=VMEM_LIMIT),
        cost_estimate=lasting(10),
        name="middle",
    )(*operands)


def halving_steps(flip):
    across, bit = [], 2
    while bit < lax.axis_size("batch"):
        across.append(("batch", bit))
        bit *= 2
    return [("blk", 1)] + across if flip else across + [("blk", 1)]


def group_of(steps, position):
    own = lax.axis_index("batch") // 2 * 2 + lax.axis_index("blk") % 2
    mask = 0
    for i, (axis, bit) in enumerate(steps):
        if position >> (len(steps) - 1 - i) & 1:
            mask += bit if axis == "batch" else 1
    return own ^ mask


def weights_kernel(*refs, steps):
    given, made, held = refs[:6], refs[6:10], refs[10:16]
    ready, square_ref, sems = refs[16:20], refs[20], refs[21]
    waiting = copies_between(given, held, sems)
    normed_ref, other_normed_ref, acts_ref, other_acts_ref, grad_ref, other_grad_ref = held
    half, lines, rows, _ = ready[0].shape
    width = square_ref.shape[1]
    span = lines * rows
    done = []

    def store(piece, part, square):
        square_ref[...] = square
        columns = slice(part * width, (part + 1) * width)
        pair = ready[2 * piece : 2 * piece + 2]
        for position in range(2 * half):
            first = pl.multiple_of(group_of(steps[piece], position) * span, span)
            shards = square_ref[pl.ds(first, span), :].astype(jnp.bfloat16).reshape(lines, rows, width)
            pair[position // half][position % half, :, :, columns] = shards
        done.extend(
            copies_between(
                [ref.at[:, :, :, pl.ds(part * width, width)] for ref in pair],
                [ref.at[:, :, :, pl.ds(part * width, width)] for ref in made[2 * piece : 2 * piece + 2]],
                sems,
                6 + len(done),
            )
        )

    for copy in waiting[:4]:
        copy.wait()
    normed_t, other_t = turned(normed_ref[...]), turned(other_normed_ref[...])
    for piece in range(2):
        for part in range(2):
            store(
                piece, part,
                project(normed_t, acts_ref[piece, part]) + project(other_t, other_acts_ref[piece, part]),
            )
        if piece == 0:
            for copy in waiting[4:]:
                copy.wait()
        store(
            piece, 2,
            over_rows(acts_ref[piece, 2], grad_ref[...])
            + over_rows(other_acts_ref[piece, 2], other_grad_ref[...]),
        )
    for copy in done:
        copy.wait()


def weight_grads(acts, normed, grad, shape, steps):
    width = normed[0].shape[1]
    count = acts[0].shape[1]
    rows = width // (shape[0] * shape[1])
    block = (shape[0] // 2, shape[1], rows, count * width)
    operands = (*normed, *acts, *grad)
    outs = [jax.ShapeDtypeStruct(block, jnp.bfloat16)] * 4
    return pl.pallas_call(
        partial(weights_kernel, steps=steps),
        in_specs=[IN_HBM] * 6,
        out_specs=[IN_HBM] * 4,
        out_shape=outs,
        scratch_shapes=held_here(operands) + held_here(outs) + [
            pltpu.VMEM((width, width), jnp.float32), pltpu.SemaphoreType.DMA((6 + 4 * count,)),
        ],
        compiler_params=pltpu.CompilerParams(vmem_limit_bytes=VMEM_LIMIT),
        cost_estimate=lasting(6),
        name="weight_grads",
    )(*operands)


def grid_of():
    return lax.axis_size("batch"), lax.axis_size("blk") // 2


def place_square(keep_ref, send_ref, square, start, shape):
    width = square.shape[1]
    half = square.shape[0] // 2
    columns = slice(start, start + width)
    parity = lax.axis_index("batch") % 2
    for h in range(2):
        shards = square[h * half : (h + 1) * half].astype(jnp.bfloat16).reshape(shape + (-1, width))

        @pl.when(parity == h)
        def _():
            keep_ref[:, :, :, columns] = shards

        @pl.when(parity != h)
        def _():
            send_ref[:, :, :, columns] = shards


def held_here(shapes):
    return [pltpu.VMEM(a.shape, a.dtype) for a in shapes]


def copies_between(sources, targets, sems, first=0):
    copies = [
        pltpu.make_async_copy(source, target, sems.at[first + i])
        for i, (source, target) in enumerate(zip(sources, targets))
    ]
    for copy in copies:
        copy.start()
    return copies


def last_kernel(*refs, sequences, rows, heads, dim, shape, count):
    width = heads * dim
    given, made, held = refs[:count], refs[count : count + 4], refs[count + 4 : 2 * count + 4]
    keep_ref, send_ref, gstates_ref, spill_ref, ext_ref, sems = refs[2 * count + 4 :]
    waiting = copies_between(given, held, sems)
    (parts_ref, normed_ref, wq_ref, wk_ref, wv_ref, att_ref, gmid_ref, joined_ref, gain_ref, ngram_ref, wjoin_ref,
     states_ref, rim_ref, start_ref, two_ref, three_ref, four_ref, ggain_ffn_ref, table_ref) = held
    done = []

    def need(*names):
        for index in names:
            waiting[index].wait()

    def give(targets, sources):
        done.extend(copies_between(sources, targets, sems, count + len(done)))

    def store(square, start):
        place_square(keep_ref, send_ref, square, start, shape)
        columns = pl.ds(start, square.shape[1])
        give(
            [ref.at[:, :, :, columns] for ref in made[:2]],
            [ref.at[:, :, :, columns] for ref in (keep_ref, send_ref)],
        )

    need(0, 1)
    normed_t = turned(normed_ref[...])
    gnormed = jnp.zeros(joined_ref.shape, jnp.float32)
    for part, w_ref in enumerate((wq_ref, wk_ref, wv_ref)):
        low = part * dim
        grad = turned(unit_columns(parts_ref, sequences, heads, low, low + dim))
        store(project(normed_t, grad), part * width)
        need(2 + part)
        gnormed = gnormed + project_back(grad, w_ref[...])
    need(5, 6)
    att_t = unit_columns(att_ref, sequences, heads, 0, dim)
    store(project(att_t, gmid_ref[...].astype(jnp.bfloat16)), 4 * width)
    need(7, 8)
    back, ggain = rms_back(
        joined_ref[...], gain_ref[...].astype(jnp.float32).reshape(1, -1), gnormed
    )
    gjoined = gmid_ref[...] + back
    gjoined_low = gjoined.astype(jnp.bfloat16)
    need(9)
    store(over_rows(ngram_ref[...], gjoined_low), 3 * width)
    need(*range(10, count))
    gngram = project_back(gjoined_low, wjoin_ref[...])
    taps = tap_rows(two_ref, three_ref, four_ref)
    gtaps = [jnp.zeros((1, width), jnp.float32)] * 4
    for s in range(sequences):
        span = slice(s * rows, (s + 1) * rows)
        states = states_ref[s].astype(jnp.float32)
        keeps = keep_columns(start_ref, s, lax.axis_index("blk") * rows, rows, width)
        ext_ref[8 - EDGE : 8, :] = rim_ref[s].astype(jnp.float32)
        ext_ref[8 : 8 + rows, :] = states
        masked = [keeps[j] * gngram[span] for j in range(4)]
        for j in range(4):
            moved = states if j == 0 else ext_ref[8 - j : 8 - j + rows, :]
            gtaps[j] = gtaps[j] + jnp.sum(masked[j] * moved, axis=0, keepdims=True)
        ext_ref[...] = jnp.zeros_like(ext_ref)
        ext_ref[8 : 8 + rows, :] = gjoined[span] + taps[0] * masked[0]
        for j in range(1, 4):
            ext_ref[8 - j : 8 - j + rows, :] += taps[j] * masked[j]
        gstates_ref[s] = ext_ref[8 : 8 + rows, :]
        spill_ref[s] = ext_ref[0:8, :]
    small = jnp.concatenate(gtaps + [ggain, ggain_ffn_ref[...], jnp.zeros((2, width), jnp.float32)], axis=0)
    lines = jnp.concatenate(
        [small[:, i * LANES : (i + 1) * LANES] for i in range(width // LANES)] + [table_ref[...]], axis=0
    )
    lines = jnp.concatenate([lines, jnp.zeros((width - lines.shape[0], LANES), jnp.float32)], axis=0)
    store(lines, 5 * width)
    give(made[2:], (gstates_ref, spill_ref))
    for copy in done:
        copy.wait()


def last(parts, att_parts, normed, joined, gmid, ngram, states, rim, starts, two, three, four,
         w_join, gain, w_query, w_key, w_value, ggain_ffn, table, heads, shape):
    sequences, rows, width = states.shape
    dim = width // heads
    shards = shape + (width // (2 * shape[0] * shape[1]), 5 * width + LANES)
    operands = (parts, normed, w_query, w_key, w_value, att_parts, gmid, joined, gain, ngram, w_join,
                states, rim, starts, two, three, four, ggain_ffn, table)
    outs = [
        jax.ShapeDtypeStruct(shards, jnp.bfloat16),
        jax.ShapeDtypeStruct(shards, jnp.bfloat16),
        jax.ShapeDtypeStruct((sequences, rows, width), jnp.float32),
        jax.ShapeDtypeStruct((sequences, 8, width), jnp.float32),
    ]
    count = len(operands)
    return pl.pallas_call(
        partial(
            last_kernel, sequences=sequences, rows=rows, heads=heads, dim=dim, shape=shape, count=count
        ),
        in_specs=[IN_HBM] * count,
        out_specs=[IN_HBM] * len(outs),
        out_shape=outs,
        scratch_shapes=held_here(operands) + held_here(outs) + [
            pltpu.VMEM((8 + rows, width), jnp.float32), pltpu.SemaphoreType.DMA((count + 14,)),
        ],
        compiler_params=pltpu.CompilerParams(vmem_limit_bytes=VMEM_LIMIT),
        cost_estimate=lasting(7),
        name="last",
    )(*operands)


def unplace_half(source, targets, held, ready, sems, side):
    count, width = len(targets), targets[0].shape[1]
    half = width // 2
    columns = [pl.ds(part * width, width) for part in range(count)]
    waiting = copies_between(
        [source.at[:, :, :, c] for c in columns], [held.at[:, :, :, c] for c in columns], sems
    )
    place = pl.ds(pl.multiple_of(side * half, half), half)
    done = []
    for part, (copy, target) in enumerate(zip(waiting, targets)):
        copy.wait()
        shards = held[:, :, :, part * width : (part + 1) * width].astype(jnp.float32)
        ready[part] = shards.reshape(half, width)
        done += copies_between((ready.at[part],), (target.at[place, :],), sems, count + part)
    return done


def unplace_own_kernel(own_ref, *refs, count):
    held, ready, sems = refs[count:]
    done = unplace_half(own_ref, refs[:count], held, ready, sems, lax.axis_index("batch") % 2)
    for copy in done:
        copy.wait()


def unplace_other_kernel(other_ref, own_lines_ref, *refs, count, buckets):
    outs = refs[count:]
    parity = lax.axis_index("batch") % 2
    width = outs[0].shape[1]
    for part, out in enumerate(outs[:count]):
        held = other_ref[:, :, :, part * width : (part + 1) * width].astype(jnp.float32)
        out[...] = held.reshape(out.shape)
    other_lines = other_ref[:, :, :, count * width :]
    lines = jnp.where(parity == 0, own_lines_ref[...], other_lines).astype(jnp.float32)
    lines = lines.reshape(-1, LANES)
    pieces = width // LANES
    small = jnp.concatenate([lines[8 * i : 8 * i + 8] for i in range(pieces)], axis=1)
    two, three, four, gain, gain_ffn, table = outs[count:]
    two[...], three[...], four[...] = small[0:2], small[0:3], small[0:4]
    gain[...], gain_ffn[...] = small[4:5], small[5:6]
    table[...] = jnp.transpose(lines[8 * pieces : 8 * pieces + buckets])[: table.shape[0]]


def half_scratch(shards, width, count):
    return held_here((shards,)) + [
        pltpu.VMEM((count, width // 2, width), jnp.float32), pltpu.SemaphoreType.DMA((2 * count,)),
    ]


def unplace_own(own, width, count):
    return pl.pallas_call(
        partial(unplace_own_kernel, count=count),
        in_specs=[IN_HBM],
        out_specs=[IN_HBM] * count,
        out_shape=[jax.ShapeDtypeStruct((width, width), jnp.float32)] * count,
        scratch_shapes=half_scratch(own, width, count),
        compiler_params=pltpu.CompilerParams(vmem_limit_bytes=VMEM_LIMIT),
        cost_estimate=lasting(2.5),
        name="unplace_own",
    )(own)


def unplace_other(other, own, squares, width, table_shape):
    count = len(squares)
    shapes = [(width, width)] * count
    shapes += [(2, width), (3, width), (4, width), (1, width), (1, width), table_shape]
    half = width // 2
    lines = pl.BlockSpec(own.shape[:3] + (LANES,), lambda i: (0, 0, 0, count * width // LANES))
    outs = [jax.ShapeDtypeStruct(shape, jnp.float32) for shape in shapes]
    parts = pl.BlockSpec((half, width), lambda i: (1 - lax.axis_index("batch") % 2, 0))
    return pl.pallas_call(
        partial(unplace_other_kernel, count=count, buckets=table_shape[1]),
        grid=(1,),
        in_specs=[whole(other.shape), lines] + [pl.BlockSpec(memory_space=pl.ANY)] * count,
        out_specs=[parts] * count + [whole(a.shape) for a in outs[count:]],
        out_shape=outs,
        input_output_aliases={2 + i: i for i in range(count)},
        compiler_params=pltpu.CompilerParams(vmem_limit_bytes=VMEM_LIMIT),
        cost_estimate=lasting(3),
        name="unplace_other",
    )(other, own, *squares)


def unplace_ffn_kernel(*refs, steps, count, given, piece, chunks):
    blocks, outs = refs[: 2 * count], refs[given : given + 3]
    held, ready, sems = refs[given + 3 : given + 3 + 2 * count], refs[given + 3 + 2 * count], refs[-1]
    waiting = copies_between(blocks, held, sems)
    lines, rows = held[0].shape[:2]
    width = ready.shape[-1]
    span = lines * rows
    done = []
    for side in range(2):
        for copy in waiting[side * count : (side + 1) * count]:
            copy.wait()
        chunk = (lax.axis_index("batch") + side) % 2 * (chunks // 2) + piece
        place = pl.ds(pl.multiple_of(chunk * width, width), width)
        for part in range(3):
            for i, block in enumerate(held[side * count : (side + 1) * count]):
                start = pl.multiple_of(group_of(steps, i) * span, span)
                shards = block[:, :, part * width : (part + 1) * width].astype(jnp.float32)
                ready[side, part, pl.ds(start, span), :] = shards.reshape(span, width)
            target = outs[part].at[place, :] if part == 2 else outs[part].at[:, place]
            done += copies_between((ready.at[side, part],), (target,), sems, 2 * count + len(done))
    for copy in done:
        copy.wait()


def unplace_ffn(blocks, steps, piece, width, hidden, chunks, before=()):
    shapes = [(width, hidden), (width, hidden), (hidden, width)]
    given = len(blocks) + len(before)
    return pl.pallas_call(
        partial(
            unplace_ffn_kernel, steps=steps, count=len(blocks) // 2, given=given, piece=piece, chunks=chunks
        ),
        in_specs=[IN_HBM] * given,
        out_specs=[IN_HBM] * 3,
        out_shape=[jax.ShapeDtypeStruct(shape, jnp.float32) for shape in shapes],
        input_output_aliases={len(blocks) + i: i for i in range(len(before))},
        scratch_shapes=held_here(blocks) + [
            pltpu.VMEM((2, 3, width, width), jnp.float32), pltpu.SemaphoreType.DMA((len(blocks) + 6,)),
        ],
        compiler_params=pltpu.CompilerParams(vmem_limit_bytes=VMEM_LIMIT),
        cost_estimate=lasting(4),
        name="unplace_ffn",
    )(*blocks, *before)


def to_line_kernel(*refs, first, second, lines):
    count = first + second
    given, made, held = refs[:count], refs[count : count + lines], refs[count + lines : 2 * count + lines]
    ready, sems = refs[2 * count + lines :]
    waiting = copies_between([ref.at[0] for ref in given], held, sems)
    wide = held[0].shape[-1]

    def total(terms):
        held_sum = terms[0][...].astype(jnp.float32)
        for term in terms[1:]:
            held_sum = held_sum + term[...].astype(jnp.float32)
        return held_sum.astype(jnp.bfloat16)

    for copy in waiting[:first]:
        copy.wait()
    ready[:, :, :wide] = total(held[:first])
    for copy in waiting[first:]:
        copy.wait()
    ready[:, :, wide:] = total(held[first:])
    own = lax.axis_index("blk") // 2
    done = copies_between([ready.at[own ^ d] for d in range(lines)], made, sems, count)
    for copy in done:
        copy.wait()


def to_line(first, second):
    lines, rows, wide = first[0].shape[1:]
    total = wide + second[0].shape[-1]
    operands = (*first, *second)
    count = len(operands)
    return pl.pallas_call(
        partial(to_line_kernel, first=len(first), second=len(second), lines=lines),
        in_specs=[IN_HBM] * count,
        out_specs=[IN_HBM] * lines,
        out_shape=[jax.ShapeDtypeStruct((rows, total), jnp.bfloat16)] * lines,
        scratch_shapes=[pltpu.VMEM(a.shape[1:], a.dtype) for a in operands] + [
            pltpu.VMEM((lines, rows, total), jnp.bfloat16), pltpu.SemaphoreType.DMA((count + lines,)),
        ],
        compiler_params=pltpu.CompilerParams(vmem_limit_bytes=VMEM_LIMIT),
        cost_estimate=lasting(3),
        name="to_line",
    )(*operands)


def from_line_kernel(*refs):
    first_ref, second_ref = refs[-2:]
    wide = first_ref.shape[-1]
    own = lax.axis_index("blk") // 2
    for d, piece in enumerate(refs[:-2]):
        first_ref[own ^ d] = piece[:, :wide]
        second_ref[own ^ d] = piece[:, wide:]


def from_line(pieces, wide):
    rows, total = pieces[0].shape
    shapes = [(len(pieces), rows, wide), (len(pieces), rows, total - wide)]
    return pl.pallas_call(
        from_line_kernel,
        grid=(1,),
        in_specs=[whole(a.shape) for a in pieces],
        out_specs=[whole(shape) for shape in shapes],
        out_shape=[jax.ShapeDtypeStruct(shape, jnp.bfloat16) for shape in shapes],
        compiler_params=pltpu.CompilerParams(vmem_limit_bytes=VMEM_LIMIT),
        cost_estimate=lasting(2),
        name="from_line",
    )(*pieces)


def traded(block, axis, bit):
    pairs = [(i, i ^ bit) for i in range(lax.axis_size(axis))]
    return lax.ppermute(block, axis, pairs)


def swapped(block):
    return traded(block, "batch", 1)


def line_traded(blocks):
    _, lines = grid_of()
    if not isinstance(blocks, (list, tuple)):
        blocks = [blocks] * (lines - 1)
    return [traded(block, "blk", 2 * (d + 1)) for d, block in enumerate(blocks)]


def added(*terms):
    total = terms[0].astype(jnp.float32)
    for term in terms[1:]:
        total = total + term.astype(jnp.float32)
    return total.astype(jnp.bfloat16)


def summed_first(parts):
    return lax.reduce(parts.astype(jnp.float32), jnp.float32(0), lax.add, (0,)).astype(jnp.bfloat16)


def over_plane(parts):
    batch, lines = grid_of()
    groups = [
        [(2 * line + p % 2) * batch + p // 2 * 2 + parity for p in range(batch)]
        for line in range(lines)
        for parity in range(2)
    ]
    return lax.all_to_all(parts, ("blk", "batch"), 0, 0, axis_index_groups=groups, tiled=True)


def over_line(parts):
    _, lines = grid_of()
    groups = [[2 * line + low for line in range(lines)] for low in range(2)]
    return lax.all_to_all(parts, "blk", 0, 0, axis_index_groups=groups, tiled=True)


def spread(block, count):
    return jnp.broadcast_to(block[None], (count,) + block.shape)


def spill_kernel(states_ref, spill_ref, out_ref):
    out_ref[...] = states_ref[...]
    for s in range(states_ref.shape[0]):
        out_ref[s, 8 - EDGE :, :] += spill_ref[s]


def add_spill(states, spill):
    sequences, rows, width = states.shape
    edge = pl.BlockSpec((sequences, 8, width), lambda i: (0, rows // 8 - 1, 0))
    return pl.pallas_call(
        spill_kernel,
        grid=(1,),
        in_specs=[edge, whole(spill.shape)],
        out_specs=edge,
        out_shape=jax.ShapeDtypeStruct(states.shape, states.dtype),
        input_output_aliases={0: 0},
        cost_estimate=lasting(1.4),
        name="add_spill",
    )(states, spill)


def exchanged(parts):
    return lax.all_to_all(parts, "blk", 0, 0, tiled=True)


def per_device(
    byte_states,
    word_start,
    bucket_of,
    conv_two,
    conv_three,
    conv_four,
    w_join,
    norm_attn,
    w_query,
    w_key,
    w_value,
    w_out,
    rel_bias,
    norm_ffn,
    w_gate,
    w_up,
    w_down,
    grad_output,
):
    sequences, block_rows, model_width = byte_states.shape
    blocks = lax.axis_size("blk")
    block_index = lax.axis_index("blk")
    head_count = rel_bias.shape[1]
    head_dim = model_width // head_count
    flat_rows = sequences * block_rows
    units = head_count * sequences
    held = units // blocks
    tile = 8 * block_rows
    shape = grid_of()
    plane, line = shape
    pin = lax.optimization_barrier
    grad_low = grad_output.reshape(flat_rows, model_width)
    other_grad = swapped(grad_low)
    rim_rows = shifted(byte_states[:, block_rows - EDGE :, :], "blk", 1)

    flipped = jnp.flip(bucket_of)
    near = block_rows - 1
    bucket_line = jnp.concatenate(
        [flipped[near:], jnp.zeros((1,), jnp.int32), flipped[:near]]
    )[None]
    joined, normed_attn, ngram_low, sent = front(
        byte_states, rim_rows, word_start, conv_two, conv_three, conv_four, w_join,
        norm_attn, w_query, w_key, w_value, head_count, blocks,
    )
    qkv = exchanged(sent)
    weight, att_sent, attended, total = attend(
        qkv, bucket_line, rel_bias.T, blocks, block_rows, head_dim, tile, sequences
    )
    att_parts = exchanged(att_sent)
    output, normed_ffn, keep_acts, send_acts, grad_mid, grad_att, ggain_ffn = middle(
        att_parts, joined, w_out, norm_ffn, w_gate, w_up, w_down, grad_low, sequences, head_count, CHUNKS
    )
    grad_parts = exchanged(grad_att)
    acts = (keep_acts, swapped(send_acts))
    normed_pair = (normed_ffn, swapped(normed_ffn))
    grad_pair = (grad_low, other_grad)
    steps_1, steps_2 = halving_steps(False), halving_steps(True)
    keep_1, out_1, keep_2, out_2 = weight_grads(acts, normed_pair, grad_pair, shape, (steps_1, steps_2))
    grad_parts, out_1, out_2 = pin((grad_parts, out_1, out_2))

    grad_qkv, grad_table = attend_back(
        qkv, weight, attended, total, grad_parts, bucket_line,
        rel_bias.shape[0], blocks, block_rows, head_dim, tile, sequences,
    )
    in_1, in_2 = traded(out_1, *steps_1[0]), traded(out_2, *steps_2[0])

    def to_send(held):
        half = held[-1].shape[0] // 2
        return added(*[h[half : 2 * half] for h in held])

    qkv_parts = exchanged(grad_qkv)
    held_1, held_2 = [keep_1, in_1], [keep_2, in_2]
    for step_1, step_2 in zip(steps_1[1:], steps_2[1:]):
        held_1.append(traded(to_send(held_1), *step_1))
        held_2.append(traded(to_send(held_2), *step_2))
    keep_3, send_3, grad_states, spill = last(
        qkv_parts, att_parts, normed_attn, joined, grad_mid, ngram_low, byte_states, rim_rows, word_start,
        conv_two, conv_three, conv_four, w_join, norm_attn, w_query, w_key, w_value, ggain_ffn,
        grad_table, head_count, shape,
    )
    send_3, held_1[-1], held_2[-1] = pin((send_3, held_1[-1], held_2[-1]))
    own_line, *out_line = to_line(held_1, held_2)
    got_3, own_line, out_line = pin((swapped(send_3), own_line, out_line))

    plane_3 = over_plane(added(keep_3, got_3))
    final = added(own_line, *line_traded(out_line))
    pieces = [final] + line_traded(final)
    plane_3, pieces = pin((plane_3, pieces))

    def gathered(held, axis, bit):
        return held + [traded(block, axis, bit) for block in held]

    def gathered_on(block, direct, steps):
        held = [block]
        for got, step in zip(direct, steps[::-1]):
            held = held + [got] + [traded(other, *step) for other in held[1:]]
        return held

    block_1, block_2 = from_line(pieces, keep_1.shape[-1])
    direct_1 = [traded(block_1, *step) for step in steps_1[::-1]]
    direct_2 = [traded(block_2, *step) for step in steps_2[::-1]]
    line_3 = over_line(summed_first(plane_3))
    direct_1, direct_2, spill = pin((direct_1, direct_2, spill))

    held_1 = gathered_on(block_1, direct_1, steps_1)
    held_2 = gathered_on(block_2, direct_2, steps_2)
    half_3 = spread(over_line(spread(summed_first(line_3), line)), plane)
    spill_rows = shifted(spill[:, 8 - EDGE :, :], "blk", -1)
    half_3, held_1, held_2, spill_rows = pin((half_3, held_1, held_2, spill_rows))
    grad_states = add_spill(grad_states, spill_rows)

    own_3 = over_plane(half_3)
    blocks_1, blocks_2 = gathered(held_1, "batch", 1), gathered(held_2, "batch", 1)
    ffn_sizes = (model_width, w_gate.shape[1], CHUNKS)
    halfway = unplace_ffn(blocks_1, steps_1, 0, *ffn_sizes)
    ffn_sums = unplace_ffn(blocks_2, steps_2, 1, *ffn_sizes, tuple(halfway))
    own_3, (gate_sum, up_sum, down_sum), grad_states = pin((own_3, tuple(ffn_sums), grad_states))

    other_3 = swapped(own_3)
    squares = unplace_own(own_3, model_width, 5)
    *squares, two, three, four, gain_sum, gain_ffn_sum, table_sum = unplace_other(
        other_3, own_3, squares, model_width, rel_bias.shape[::-1]
    )
    query_sum, key_sum, value_sum, join_sum, out_sum = squares
    return (
        output.reshape(byte_states.shape),
        grad_states,
        two,
        three,
        four,
        join_sum,
        gain_sum[0],
        query_sum,
        key_sum,
        value_sum,
        out_sum,
        table_sum.T,
        gain_ffn_sum[0],
        gate_sum,
        up_sum,
        down_sum,
    )


def solution(mesh):
    return jax.shard_map(
        per_device,
        mesh=mesh,
        in_specs=(
            P("batch", "blk", None),
            P("batch", "blk"),
            P(),
            P(),
            P(),
            P(),
            P(),
            P(),
            P(),
            P(),
            P(),
            P(),
            P(),
            P(),
            P(),
            P(),
            P(),
            P("batch", "blk", None),
        ),
        out_specs=(
            P("batch", "blk", None),
            P("batch", "blk", None),
            P(),
            P(),
            P(),
            P(),
            P(),
            P(),
            P(),
            P(),
            P(),
            P(),
            P(),
            P(),
            P(),
            P(),
        ),
        check_vma=False,
    )
```
